128 devices in a mesh: grp: 2 (over x_hi), seq: 64 (over z, x_lo, y, core).
Axes of the slice: x: 4 (x_hi: 2, x_lo: 2; x = x_hi * 2 + x_lo), y: 4, z: 4, core: 2. Of those that a mesh axis runs over, the one named last changes fastest.
Arguments:
- queries: bfloat16 [32, 16384, 128], P(None, ('grp', 'seq')), may hold values from -5 to 5
- keys: bfloat16 [32, 16384, 128], P(None, ('grp', 'seq')), may hold values from -5 to 5
- values: bfloat16 [32, 16384, 128], P(None, ('grp', 'seq')), may hold values from -4 to 4
- tiles: int32 [128, 32, 38], P(('grp', 'seq')), may hold values from 0 to 127, as said below
Outputs:
- attended: bfloat16 [32, 16384, 128], P(None, ('grp', 'seq'))
The draws below stay inside these ranges and needn't reach their ends.
Inputs may be any that keep to these rules, and one draw needn't show every extreme that they name: `tiles`: for every query band and head, columns g * 19 to (g + 1) * 19 - 1 name 19 different key bands, all from g * 64 to (g + 1) * 64 - 1.
All inputs are finite; a program needn't handle non-finite values.
Results may differ from the reference program's by a relative error of at most 0.005.
Values may be sent and summed in bfloat16 or wider, within the bound.
A program may use at most 128 MiB of HBM per device.

```python
import jax
import jax.numpy as jnp
from jax import lax

HEADS = 32
HEAD_DIM = 128
BAND = 128
GROUP_BANDS = 64
PER_GROUP = 19
LISTED = 38
QBANDS = 128
TOKENS = 16384
N_GRP = 2


def base_field(key):
    return jnp.clip(1.6 * jax.random.normal(key, (HEADS, TOKENS, HEAD_DIM), jnp.float32), -5.0, 5.0)


def draw_queries(key, part):
    drawn_field = base_field(jax.random.fold_in(key, 1))
    return drawn_field.astype(jnp.bfloat16)


def draw_keys(key, part):
    drawn_field = base_field(jax.random.fold_in(key, 2))
    return drawn_field.astype(jnp.bfloat16)


def draw_tiles(key, part):
    raw_scores = jax.random.randint(key, (QBANDS, HEADS, N_GRP, GROUP_BANDS), 0, 1 << 20)
    scores = raw_scores * GROUP_BANDS + jnp.arange(GROUP_BANDS)
    ignored, picked = lax.top_k(scores, PER_GROUP)
    picked = picked + (jnp.arange(N_GRP) * GROUP_BANDS)[:, None]
    return picked.reshape(QBANDS, HEADS, LISTED).astype(jnp.int32)


def block_scale(stream_key, extent, pieces, least, top_value):
    loudness = 1.0
    for axis_at, parts in pieces:
        steps = jax.random.uniform(jax.random.fold_in(jax.random.fold_in(stream_key, 6), axis_at), (parts,), jnp.float32, least / len(pieces), top_value / len(pieces))
        loudness = loudness * jnp.repeat(jnp.exp(steps), extent[axis_at] // parts).reshape((-1,) + (1,) * (len(extent) - 1 - axis_at))
    return loudness


def gaussian(key, shape, deviation, most, shards=(), held_as=jnp.bfloat16):
    factor_of = block_scale(key, shape, shards, -0.22, 0.18) if shards else 1.0
    entries = jax.random.normal(key, shape, jnp.float32) * deviation * factor_of
    return jnp.minimum(jnp.maximum(entries, -most), most).astype(held_as)


def setup_inputs(seed: int = 0) -> dict:
    streams_of = jax.random.split(jax.random.key(seed), 5)
    return {
        "queries": draw_queries(jax.random.fold_in(streams_of[4], 71), 0),
        "keys": draw_keys(jax.random.fold_in(streams_of[4], 71), 0),
        "values": gaussian(streams_of[2], (HEADS, TOKENS, HEAD_DIM), 1.0, 4.0, ((1, 128),)),
        "tiles": draw_tiles(jax.random.fold_in(streams_of[4], 71), 0),
    }


def one_head(operands):
    head_queries, head_keys, head_values, head_tiles = operands
    band_queries = head_queries.reshape(QBANDS, BAND, HEAD_DIM).astype(jnp.float32)
    key_bands = head_keys.reshape(QBANDS, BAND, HEAD_DIM)
    value_bands = head_values.reshape(QBANDS, BAND, HEAD_DIM)
    picked_keys = key_bands[head_tiles].reshape(QBANDS, LISTED * BAND, HEAD_DIM).astype(jnp.float32)
    picked_values = value_bands[head_tiles].reshape(QBANDS, LISTED * BAND, HEAD_DIM).astype(jnp.float32)
    scores = jnp.einsum("qrd,qkd->qrk", band_queries, picked_keys) * (HEAD_DIM ** -0.5)
    row_max = jnp.max(scores, axis=-1, keepdims=True)
    weights = jnp.exp(scores - row_max)
    row_sum = jnp.sum(weights, axis=-1, keepdims=True)
    rounded = lax.optimization_barrier(weights.astype(jnp.bfloat16)).astype(jnp.float32)
    mixed = jnp.einsum("qrk,qkd->qrd", rounded, picked_values) / row_sum
    return mixed.astype(jnp.bfloat16).reshape(QBANDS * BAND, HEAD_DIM)


def reference(queries, keys, values, tiles):
    head_tiles = jnp.transpose(tiles, (1, 0, 2))
    return lax.map(one_head, (queries, keys, values, head_tiles))
```

```python
import functools

import jax
import jax.numpy as jnp
from jax import lax
from jax.experimental import pallas as pl
from jax.experimental.pallas import tpu as pltpu
from jax.sharding import PartitionSpec as P

MESH = pl.DeviceIdType.MESH
BAND = 128
WIDTH = 128
HEADS = 32
PER = 19
SCALE = 128.0**-0.5 * 1.4426950408889634
NT = (((1,), (1,)), ((), ()))
COLS = [list(range(i, min(PER, i + 2))) for i in range(0, PER, 2)]


def device(x, y, z, c):
    return (x // 2, ((z * 2 + x % 2) * 4 + y) * 2 + c)


def kernel(
    q_ref, k_ref, v_ref, tiles_ref, o_ref,
    own_kv, far_kv, queries, lists_out, lists_in, lists, scores, maxima, acc_own, max_own, mixed,
    send_kv, send_lists, send_fwd, send_out,
    got_direct, got_partner, got_sibling, got_relayed, got_queries, got_lists, got_out, lists_sem,
):
    s = lax.axis_index("seq")
    pair = lax.axis_index("grp")
    c = s % 2
    y = (s // 2) % 4
    x_lo = (s // 8) % 2
    z = s // 16
    x = pair * 2 + x_lo
    beside = 3 - x
    sibling = device(x, y, z, 1 - c)
    partner = device(x + 1 - 2 * x_lo, y, z, c)
    own_head = pair * 16 + z * 4 + y
    own_part = (x_lo * 2 + c) * 16
    far_part = ((1 - x_lo) * 2 + c) * 16

    t = tiles_ref[0]
    head = lax.broadcasted_iota(jnp.int32, t.shape, 0)
    dy_of = ((head & 3) - ((t >> 1) & 3)) & 3
    dz_of = (((head >> 2) & 3) - ((t >> 4) & 3)) & 3
    slot_of = (((t >> 3) & 1) * 2 + (t & 1)) * 16 + ((dz_of - dy_of) & 3) * 4 + dy_of
    slot_of = jnp.concatenate([slot_of, jnp.zeros((HEADS, 128 - 2 * PER), jnp.int32)], 1)
    for h in range(HEADS):
        lists_out[h] = slot_of[h : h + 1]

    def target(i):
        dy = i % 4
        dz = (i // 4 + dy) % 4
        return (y + dy) % 4, (z + dz) % 4

    def remote(src, dst, send_sem, recv_sem, device_id):
        return pltpu.make_async_remote_copy(
            src_ref=src, dst_ref=dst, send_sem=send_sem, recv_sem=recv_sem, device_id=device_id, device_id_type=MESH
        )

    def send_lists_to(i, own):
        ty, tz = target(i)
        if own:
            remote(lists_out.at[pair * 16 + tz * 4 + ty], lists_in.at[i], send_lists, got_lists, device(x, ty, tz, c)).start()
        remote(
            lists_out.at[(1 - pair) * 16 + tz * 4 + ty], lists_in.at[16 + i], send_lists, got_lists, device(beside, ty, tz, c)
        ).start()

    def send_kv_to(i, own):
        ty, tz = target(i)
        here, there = pair * 16 + tz * 4 + ty, (1 - pair) * 16 + tz * 4 + ty
        for which, ref in ((0, k_ref), (1, v_ref)):
            if own:
                remote(
                    ref.at[here], own_kv.at[own_part + i, which], send_kv, got_direct.at[0, i // 4], device(x, ty, tz, c)
                ).start()
            remote(
                ref.at[there], far_kv.at[own_part + i, which], send_kv, got_direct.at[1, i // 4], device(beside, ty, tz, c)
            ).start()

    def send_queries_to(i, own):
        ty, tz = target(i)
        if own:
            remote(q_ref.at[pair * 16 + tz * 4 + ty], queries.at[i], send_kv, got_queries, device(x, ty, tz, c)).start()
        remote(
            q_ref.at[(1 - pair) * 16 + tz * 4 + ty], queries.at[16 + i], send_kv, got_queries, device(beside, ty, tz, c)
        ).start()

    def each_offset(step):
        step(0, False)

        def body(i, carry):
            step(i, True)
            return carry

        lax.fori_loop(1, 16, body, 0)

    pltpu.make_async_copy(k_ref.at[own_head], own_kv.at[own_part, 0], got_direct.at[0, 0]).start()
    pltpu.make_async_copy(v_ref.at[own_head], own_kv.at[own_part, 1], got_direct.at[0, 0]).start()
    pltpu.make_async_copy(q_ref.at[own_head], queries.at[0], got_queries).start()
    pltpu.make_async_copy(lists_out.at[own_head], lists_in.at[0], got_lists).start()
    each_offset(send_lists_to)
    each_offset(send_kv_to)
    each_offset(send_queries_to)

    def chunk(ref, part, j):
        return ref.at[pl.ds(part + j * 4, 4)]

    def arrived(view, sem):
        pltpu.make_async_copy(view, view, sem).wait()

    def pass_on(ref, part, plane, j):
        view = chunk(ref, part, j)
        arrived(view, got_direct.at[plane, j])
        remote(view, view, send_fwd, got_partner.at[plane, j], partner).start()
        remote(view, view, send_fwd, got_sibling.at[plane], sibling).start()

    def relay(ref, part, plane, j):
        view = chunk(ref, part, j)
        arrived(view, got_partner.at[plane, j])
        remote(view, view, send_fwd, got_relayed.at[plane], sibling).start()

    def four(step):
        def body(j, carry):
            step(j)
            return carry

        lax.fori_loop(0, 4, body, 0)

    four(lambda j: pass_on(own_kv, own_part, 0, j))
    four(lambda j: pass_on(far_kv, far_part, 1, j))
    four(lambda j: relay(own_kv, far_part, 0, j))
    arrived(lists_in, got_lists)
    copy_lists = pltpu.make_async_copy(lists_in, lists, lists_sem)
    copy_lists.start()
    copy_lists.wait()
    arrived(queries, got_queries)
    part = own_kv.at[pl.ds(0, 16)]
    arrived(part, got_sibling.at[0])
    arrived(part, got_relayed.at[0])

    def attend(kv, base, finish, between):
        def step(new, new_slot, old, old_slot):
            running = acc = None
            if new is not None:
                query = queries[new]
            if old is not None:
                shift = maxima[old_slot]
            for cols in COLS:
                span = pl.ds(cols[0] * BAND, len(cols) * BAND)
                if new is not None:
                    keys = jnp.concatenate([kv[lists[new, 0, base + col], 0] for col in cols], 0)
                    found = lax.dot_general(query, keys, NT, preferred_element_type=jnp.float32)
                    scores[new_slot, :, span] = found
                    for n in range(len(cols)):
                        piece = found[:, n * BAND : (n + 1) * BAND]
                        running = piece if running is None else jnp.maximum(running, piece)
                if old is not None:
                    values = jnp.concatenate([kv[lists[old, 0, base + col], 1] for col in cols], 0)
                    values = jnp.concatenate([values, jnp.ones_like(values)], 1)
                    weights = jnp.exp2(scores[old_slot, :, span] * SCALE - jnp.concatenate([shift] * len(cols), 1))
                    product = jnp.dot(weights.astype(jnp.bfloat16), values, preferred_element_type=jnp.float32)
                    acc = product if acc is None else acc + product
            if new is not None:
                maxima[new_slot] = jnp.broadcast_to(jnp.max(running, -1, keepdims=True) * SCALE, (BAND, BAND))
            if old is not None:
                finish(old, shift, acc)

        step(0, 0, None, None)

        def body(i, carry):
            step(2 * i + 1, 1, 2 * i, 0)
            step(jnp.minimum(2 * i + 2, 31), 0, 2 * i + 1, 1)
            between(i)
            return carry

        lax.fori_loop(0, 16, body, 0)

    def keep(unit, shift, acc):
        acc_own[unit] = acc
        max_own[unit] = shift

    def relay_between(i):
        @pl.when(i % 4 == 3)
        def _():
            relay(far_kv, own_part, 1, i // 4)

    attend(own_kv, pair * PER, keep, relay_between)

    part = far_kv.at[pl.ds(0, 16)]
    arrived(part, got_sibling.at[1])
    arrived(part, got_relayed.at[1])

    def merge(unit, shift, acc):
        first, first_shift = acc_own[unit], max_own[unit]
        joint = jnp.maximum(shift, first_shift)
        now, before = jnp.exp2(shift - joint), jnp.exp2(first_shift - joint)
        top = acc[:, :WIDTH] * now + first[:, :WIDTH] * before
        bottom = acc[:, WIDTH:] * now + first[:, WIDTH:] * before
        mixed[unit] = (top / bottom).astype(jnp.bfloat16)

    def give_back(unit):
        i = unit % 16
        dy = i % 4
        dz = (i // 4 + dy) % 4
        plane = jnp.where(unit < 16, x, beside)
        remote(
            mixed.at[unit], o_ref.at[own_head], send_out, got_out,
            device(plane, (y - dy + 4) % 4, (z - dz + 4) % 4, c),
        ).start()

    def give_two(i):
        @pl.when(i == 0)
        def _():
            pltpu.make_async_copy(mixed.at[0], o_ref.at[own_head], got_out).start()

        @pl.when(i > 0)
        def _():
            give_back(2 * i)

        give_back(2 * i + 1)

    attend(far_kv, (1 - pair) * PER, merge, give_two)

    def sent(view, sem):
        pltpu.make_async_copy(view, view, sem).wait()

    arrived(o_ref, got_out)
    sent(o_ref.at[pl.ds(0, 31)], send_out)
    sent(lists_out.at[pl.ds(0, 31)], send_lists)
    sent(own_kv.at[pl.ds(0, 31)], send_kv)
    sent(queries.at[pl.ds(0, 31)], send_kv)
    sent(own_kv, send_fwd)
    sent(own_kv.at[pl.ds(0, 32)], send_fwd)


def on_device(queries, keys, values, tiles):
    dma = pltpu.SemaphoreType.DMA
    any_space = pl.BlockSpec(memory_space=pl.ANY)
    bf16, f32 = jnp.bfloat16, jnp.float32
    return pl.pallas_call(
        kernel,
        out_shape=jax.ShapeDtypeStruct((HEADS, BAND, WIDTH), bf16),
        in_specs=[any_space, any_space, any_space, pl.BlockSpec(memory_space=pltpu.VMEM)],
        out_specs=any_space,
        scratch_shapes=[
            pltpu.VMEM((64, 2, BAND, WIDTH), bf16),
            pltpu.VMEM((64, 2, BAND, WIDTH), bf16),
            pltpu.VMEM((32, BAND, WIDTH), bf16),
            pltpu.VMEM((HEADS, 1, 128), jnp.int32),
            pltpu.VMEM((32, 1, 128), jnp.int32),
            pltpu.SMEM((32, 1, 128), jnp.int32),
            pltpu.VMEM((2, BAND, PER * BAND), f32),
            pltpu.VMEM((2, BAND, BAND), f32),
            pltpu.VMEM((32, BAND, 2 * WIDTH), f32),
            pltpu.VMEM((32, BAND, BAND), f32),
            pltpu.VMEM((32, BAND, WIDTH), bf16),
            dma, dma, dma, dma,
            dma((2, 4)), dma((2, 4)), dma((2,)), dma((2,)), dma, dma, dma, dma,
        ],
        compiler_params=pltpu.CompilerParams(has_side_effects=True, vmem_limit_bytes=52 * 2**20),
        cost_estimate=pl.CostEstimate(flops=10_200_000_000, bytes_accessed=4 * 2**20, transcendentals=20_000_000),
        name="attend_listed",
    )(queries, keys, values, tiles)


def solution(mesh):
    return jax.shard_map(
        on_device,
        mesh=mesh,
        in_specs=(
            P(None, ("grp", "seq"), None),
            P(None, ("grp", "seq"), None),
            P(None, ("grp", "seq"), None),
            P(("grp", "seq"), None, None),
        ),
        out_specs=P(None, ("grp", "seq"), None),
        check_vma=False,
    )
```

```python
import functools

import jax
import jax.numpy as jnp
from jax import lax
from jax.experimental import pallas as pl
from jax.experimental.pallas import tpu as pltpu
from jax.sharding import PartitionSpec as P

MESH = pl.DeviceIdType.MESH
BAND = 128
WIDTH = 128
HEADS = 32
PER = 19
SCALE = 128.0**-0.5 * 1.4426950408889634
NT = (((1,), (1,)), ((), ()))
OWN_K, OWN_V, FAR_K, FAR_V = range(4)
STEP = 8
COLS = [list(range(i, min(PER, i + 2))) for i in range(0, PER, 2)]


def device(x, y, z, c):
    return (x // 2, ((z * 2 + x % 2) * 4 + y) * 2 + c)


def kernel(
    q_ref, k_ref, v_ref, tiles_ref, o_ref,
    own_k, own_v, far_k, far_v, queries, lists_out, lists_in, lists, weights, acc_own, max_own, max_far, mixed,
    send_kv, send_lists, send_fwd, send_out,
    got_direct, got_partner, got_sibling, got_relayed, got_queries, got_lists, got_out, lists_sem,
):
    s = lax.axis_index("seq")
    pair = lax.axis_index("grp")
    c = s % 2
    y = (s // 2) % 4
    x_lo = (s // 8) % 2
    z = s // 16
    x = pair * 2 + x_lo
    beside = 3 - x
    sibling = device(x, y, z, 1 - c)
    partner = device(x + 1 - 2 * x_lo, y, z, c)
    own_head = pair * 16 + z * 4 + y
    own_part = (x_lo * 2 + c) * 16
    far_part = ((1 - x_lo) * 2 + c) * 16

    def target(i):
        dy = i % 4
        dz = (i // 4 + dy) % 4
        return (y + dy) % 4, (z + dz) % 4

    barrier = pltpu.get_barrier_semaphore()

    def greet(device_id):
        pl.semaphore_signal(barrier, inc=1, device_id=device_id, device_id_type=MESH)

    greet(sibling)
    greet(partner)
    greet(device(beside, y, z, c))

    def greet_both(i, carry):
        ty, tz = target(i)
        greet(device(x, ty, tz, c))
        greet(device(beside, ty, tz, c))
        return carry

    lax.fori_loop(1, 16, greet_both, 0)

    t = tiles_ref[0]
    head = lax.broadcasted_iota(jnp.int32, t.shape, 0)
    dy_of = ((head & 3) - ((t >> 1) & 3)) & 3
    dz_of = (((head >> 2) & 3) - ((t >> 4) & 3)) & 3
    slot_of = (((t >> 3) & 1) * 2 + (t & 1)) * 16 + ((dz_of - dy_of) & 3) * 4 + dy_of
    slot_of = jnp.concatenate([slot_of, jnp.zeros((HEADS, 128 - 2 * PER), jnp.int32)], 1)
    for h in range(HEADS):
        lists_out[h] = slot_of[h : h + 1]

    def remote(src, dst, send_sem, recv_sem, device_id):
        return pltpu.make_async_remote_copy(
            src_ref=src, dst_ref=dst, send_sem=send_sem, recv_sem=recv_sem, device_id=device_id, device_id_type=MESH
        )

    def send_lists_to(i, own):
        ty, tz = target(i)
        if own:
            remote(
                lists_out.at[pair * 16 + tz * 4 + ty], lists_in.at[16 + i], send_lists, got_lists, device(x, ty, tz, c)
            ).start()
        remote(
            lists_out.at[(1 - pair) * 16 + tz * 4 + ty], lists_in.at[i], send_lists, got_lists, device(beside, ty, tz, c)
        ).start()

    def send_own(kind, ref):
        def step(i, away):
            ty, tz = target(i)
            src, dst = ref.at[pair * 16 + tz * 4 + ty], stores[kind].at[own_part + i]
            if away:
                remote(src, dst, send_kv, got_direct.at[kind, i // 4], device(x, ty, tz, c)).start()
            else:
                pltpu.make_async_copy(src, dst, got_direct.at[kind, 0]).start()

        return step

    def send_far(kind, ref):
        def step(i, away):
            ty, tz = target(i)
            src, dst = ref.at[(1 - pair) * 16 + tz * 4 + ty], stores[kind].at[own_part + i]
            remote(src, dst, send_kv, got_direct.at[kind, i // 4], device(beside, ty, tz, c)).start()

        return step

    def send_own_queries(i, away):
        ty, tz = target(i)
        src = q_ref.at[pair * 16 + tz * 4 + ty]
        if away:
            remote(src, queries.at[16 + i], send_kv, got_queries.at[1 + i // 4], device(x, ty, tz, c)).start()
        else:
            pltpu.make_async_copy(src, queries.at[16], got_queries.at[1]).start()

    def send_far_queries(i, away):
        ty, tz = target(i)
        src = q_ref.at[(1 - pair) * 16 + tz * 4 + ty]
        remote(src, queries.at[i], send_kv, got_queries.at[0], device(beside, ty, tz, c)).start()

    def each_offset(*steps):
        for step in steps:
            step(0, False)

        def body(i, carry):
            for step in steps:
                step(i, True)
            return carry

        lax.fori_loop(1, 16, body, 0)

    stores = (own_k, own_v, far_k, far_v)
    arriving = (own_part, own_part, far_part, far_part)
    relaying = (far_part, far_part, own_part, own_part)
    pltpu.make_async_copy(lists_out.at[own_head], lists_in.at[16], got_lists).start()
    pl.semaphore_wait(barrier, 33)
    each_offset(send_own(OWN_K, k_ref))
    each_offset(send_lists_to)
    each_offset(send_far_queries, send_own(OWN_V, v_ref))

    def arrived(view, sem):
        pltpu.make_async_copy(view, view, sem).wait()

    def pass_on(kind, j):
        view = stores[kind].at[pl.ds(arriving[kind] + j * 4, 4)]
        arrived(view, got_direct.at[kind, j])
        remote(view, view, send_fwd, got_partner.at[kind, j], partner).start()
        remote(view, view, send_fwd, got_sibling.at[kind], sibling).start()

    def relay(kind, j):
        view = stores[kind].at[pl.ds(relaying[kind] + j * 4, 4)]
        arrived(view, got_partner.at[kind, j])
        remote(view, view, send_fwd, got_relayed.at[kind], sibling).start()

    def complete(kind):
        view = stores[kind].at[pl.ds(0, 16)]
        arrived(view, got_sibling.at[kind])
        arrived(view, got_relayed.at[kind])

    def attend(kind, shifts, events):
        def one(unit):
            query = queries[unit]
            running, found = None, []
            for cols in COLS:
                keys = jnp.concatenate([stores[kind][lists[unit, 0, bases[kind] + col]] for col in cols], 0)
                found.append(lax.dot_general(query, keys, NT, preferred_element_type=jnp.float32))
                for n in range(len(cols)):
                    piece = found[-1][:, n * BAND : (n + 1) * BAND]
                    running = piece if running is None else jnp.maximum(running, piece)
            shift = jnp.broadcast_to(jnp.max(running, -1, keepdims=True) * SCALE, (BAND, BAND))
            shifts[unit] = shift
            for cols, score in zip(COLS, found):
                weight = jnp.exp2(score * SCALE - jnp.concatenate([shift] * len(cols), 1))
                weights[unit, :, pl.ds(cols[0] * BAND, len(cols) * BAND)] = weight.astype(jnp.bfloat16)

        units(one, events)

    def mix(kind, finish, events, after=None):
        def one(unit):
            acc = None
            for cols in COLS:
                values = jnp.concatenate([stores[kind][lists[unit, 0, bases[kind] + col]] for col in cols], 0)
                values = jnp.concatenate([values, jnp.ones_like(values)], 1)
                weight = weights[unit, :, pl.ds(cols[0] * BAND, len(cols) * BAND)]
                product = jnp.dot(weight, values, preferred_element_type=jnp.float32)
                acc = product if acc is None else acc + product
            finish(unit, acc)

        units(one, events, after)

    def units(one, events, after=None):
        def body(i, carry):
            for at, event in events:
                pl.when(i == at)(event)
            for n in range(STEP):
                one(i * STEP + n)
            if after is not None:
                for n in range(STEP):
                    after(i * STEP + n)
            return carry

        lax.fori_loop(0, 32 // STEP, body, 0)

    def passing(at, kind, j):
        return at, functools.partial(pass_on, kind, j)

    def relaying_at(at, kind, j):
        return at, functools.partial(relay, kind, j)

    bases = (pair * PER, pair * PER, (1 - pair) * PER, (1 - pair) * PER)
    for j in range(4):
        pass_on(OWN_K, j)
    each_offset(send_far(FAR_K, k_ref), send_own_queries)
    each_offset(send_far(FAR_V, v_ref))
    for j in range(3):
        pass_on(OWN_V, j)
        relay(OWN_K, j)
    arrived(lists_in, got_lists)
    copy_lists = pltpu.make_async_copy(lists_in, lists, lists_sem)
    copy_lists.start()
    copy_lists.wait()
    pass_on(OWN_V, 3)
    relay(OWN_K, 3)
    arrived(queries.at[pl.ds(0, 16)], got_queries.at[0])
    complete(OWN_K)

    def more_queries(at, j):
        return at, lambda: arrived(queries.at[pl.ds(16 + j * 4, 4)], got_queries.at[1 + j])

    attend(
        OWN_K,
        max_own,
        [
            passing(1, FAR_K, 0), relaying_at(1, OWN_V, 0), more_queries(2, 0), passing(2, FAR_K, 1), more_queries(2, 1),
            relaying_at(2, OWN_V, 1), passing(3, FAR_K, 2), more_queries(3, 2), relaying_at(3, OWN_V, 2),
            more_queries(3, 3), relaying_at(3, OWN_V, 3),
        ],
    )
    complete(OWN_V)

    def keep(unit, acc):
        acc_own[unit] = acc

    mix(
        OWN_V,
        keep,
        [
            passing(0, FAR_K, 3), relaying_at(1, FAR_K, 0), passing(2, FAR_V, 0), relaying_at(2, FAR_K, 1),
            passing(3, FAR_V, 1), relaying_at(3, FAR_K, 2),
        ],
    )
    pass_on(FAR_V, 2)
    pass_on(FAR_V, 3)
    relay(FAR_K, 3)
    complete(FAR_K)
    attend(
        FAR_K,
        max_far,
        [relaying_at(1, FAR_V, 0), relaying_at(2, FAR_V, 1), relaying_at(3, FAR_V, 2)],
    )
    relay(FAR_V, 3)
    complete(FAR_V)

    def merge(unit, acc):
        first, shift, first_shift = acc_own[unit], max_far[unit], max_own[unit]
        joint = jnp.maximum(shift, first_shift)
        now, before = jnp.exp2(shift - joint), jnp.exp2(first_shift - joint)
        top = acc[:, :WIDTH] * now + first[:, :WIDTH] * before
        bottom = acc[:, WIDTH:] * now + first[:, WIDTH:] * before
        mixed[unit] = (top / bottom).astype(jnp.bfloat16)

    def give_back(unit):
        i = unit % 16
        dy = i % 4
        dz = (i // 4 + dy) % 4
        plane = jnp.where(unit < 16, beside, x)

        @pl.when(unit == 16)
        def _():
            pltpu.make_async_copy(mixed.at[16], o_ref.at[own_head], got_out).start()

        @pl.when(unit != 16)
        def _():
            remote(
                mixed.at[unit], o_ref.at[own_head], send_out, got_out,
                device(plane, (y - dy + 4) % 4, (z - dz + 4) % 4, c),
            ).start()

    mix(FAR_V, merge, [], give_back)

    def sent(view, sem):
        pltpu.make_async_copy(view, view, sem).wait()

    arrived(o_ref, got_out)
    sent(o_ref.at[pl.ds(0, 31)], send_out)
    sent(lists_out.at[pl.ds(0, 31)], send_lists)
    for store in stores[:2]:
        sent(store.at[pl.ds(0, 31)], send_kv)
    sent(queries.at[pl.ds(0, 31)], send_kv)
    for store in stores:
        sent(store.at[pl.ds(0, 48)], send_fwd)


def on_device(queries, keys, values, tiles):
    dma = pltpu.SemaphoreType.DMA
    any_space = pl.BlockSpec(memory_space=pl.ANY)
    bf16, f32 = jnp.bfloat16, jnp.float32
    return pl.pallas_call(
        kernel,
        out_shape=jax.ShapeDtypeStruct((HEADS, BAND, WIDTH), bf16),
        in_specs=[any_space, any_space, any_space, pl.BlockSpec(memory_space=pltpu.VMEM)],
        out_specs=any_space,
        scratch_shapes=[
            pltpu.VMEM((64, BAND, WIDTH), bf16),
            pltpu.VMEM((64, BAND, WIDTH), bf16),
            pltpu.VMEM((64, BAND, WIDTH), bf16),
            pltpu.VMEM((64, BAND, WIDTH), bf16),
            pltpu.VMEM((32, BAND, WIDTH), bf16),
            pltpu.VMEM((HEADS, 1, 128), jnp.int32),
            pltpu.VMEM((32, 1, 128), jnp.int32),
            pltpu.SMEM((32, 1, 128), jnp.int32),
            pltpu.VMEM((32, BAND, PER * BAND), bf16),
            pltpu.VMEM((32, BAND, 2 * WIDTH), f32),
            pltpu.VMEM((32, BAND, BAND), f32),
            pltpu.VMEM((32, BAND, BAND), f32),
            pltpu.VMEM((32, BAND, WIDTH), bf16),
            dma, dma, dma, dma,
            dma((4, 4)), dma((4, 4)), dma((4,)), dma((4,)), dma((5,)), dma, dma, dma,
        ],
        compiler_params=pltpu.CompilerParams(collective_id=0, has_side_effects=True, vmem_limit_bytes=52 * 2**20),
        cost_estimate=pl.CostEstimate(flops=10_200_000_000, bytes_accessed=4 * 2**20, transcendentals=20_000_000),
        name="attend_listed",
    )(queries, keys, values, tiles)


def solution(mesh):
    return jax.shard_map(
        on_device,
        mesh=mesh,
        in_specs=(
            P(None, ("grp", "seq"), None),
            P(None, ("grp", "seq"), None),
            P(None, ("grp", "seq"), None),
            P(("grp", "seq"), None, None),
        ),
        out_specs=P(None, ("grp", "seq"), None),
        check_vma=False,
    )
```

```python
import functools

import jax
import jax.numpy as jnp
from jax import lax
from jax.experimental import pallas as pl
from jax.experimental.pallas import tpu as pltpu
from jax.sharding import PartitionSpec as P

MESH = pl.DeviceIdType.MESH
BAND = 128
WIDTH = 128
HEADS = 32
PER = 19
SCALE = 128.0**-0.5 * 1.4426950408889634
NT = (((1,), (1,)), ((), ()))
OWN_K, OWN_V, FAR_K, FAR_V = range(4)
STEP = 8
COLS = [list(range(i, min(PER, i + 2))) for i in range(0, PER, 2)]


def device(x, y, z, c):
    return (x // 2, ((z * 2 + x % 2) * 4 + y) * 2 + c)


def kernel(
    q_ref, k_ref, v_ref, tiles_ref, o_ref,
    own_k, own_v, far_k, far_v, queries, lists_out, lists_in, lists, weights_own, weights_far, acc_own, max_own,
    send_kv, send_lists, send_fwd, send_out,
    got_direct, got_partner, got_sibling, got_relayed, got_queries, got_lists, got_out, lists_sem,
):
    s = lax.axis_index("seq")
    pair = lax.axis_index("grp")
    c = s % 2
    y = (s // 2) % 4
    x_lo = (s // 8) % 2
    z = s // 16
    x = pair * 2 + x_lo
    beside = 3 - x
    sibling = device(x, y, z, 1 - c)
    partner = device(x + 1 - 2 * x_lo, y, z, c)
    own_head = pair * 16 + z * 4 + y
    own_part = (x_lo * 2 + c) * 16
    far_part = ((1 - x_lo) * 2 + c) * 16

    def target(i):
        dy = i % 4
        dz = (i // 4 + dy) % 4
        return (y + dy) % 4, (z + dz) % 4

    barrier = pltpu.get_barrier_semaphore()

    def greet(device_id):
        pl.semaphore_signal(barrier, inc=1, device_id=device_id, device_id_type=MESH)

    greet(sibling)
    greet(partner)
    greet(device(beside, y, z, c))

    def greet_both(i, carry):
        ty, tz = target(i)
        greet(device(x, ty, tz, c))
        greet(device(beside, ty, tz, c))
        return carry

    lax.fori_loop(1, 16, greet_both, 0)

    t = tiles_ref[0]
    head = lax.broadcasted_iota(jnp.int32, t.shape, 0)
    dy_of = ((head & 3) - ((t >> 1) & 3)) & 3
    dz_of = (((head >> 2) & 3) - ((t >> 4) & 3)) & 3
    slot_of = (((t >> 3) & 1) * 2 + (t & 1)) * 16 + ((dz_of - dy_of) & 3) * 4 + dy_of
    slot_of = jnp.concatenate([slot_of, jnp.zeros((HEADS, 128 - 2 * PER), jnp.int32)], 1)
    for h in range(HEADS):
        lists_out[h] = slot_of[h : h + 1]

    def remote(src, dst, send_sem, recv_sem, device_id):
        return pltpu.make_async_remote_copy(
            src_ref=src, dst_ref=dst, send_sem=send_sem, recv_sem=recv_sem, device_id=device_id, device_id_type=MESH
        )

    def send_lists_to(i, away):
        ty, tz = target(i)
        if away:
            remote(
                lists_out.at[pair * 16 + tz * 4 + ty], lists_in.at[i], send_lists, got_lists, device(x, ty, tz, c)
            ).start()
        remote(
            lists_out.at[(1 - pair) * 16 + tz * 4 + ty], lists_in.at[16 + i], send_lists, got_lists, device(beside, ty, tz, c)
        ).start()

    def send_own(kind, ref):
        def step(i, away):
            ty, tz = target(i)
            src, dst = ref.at[pair * 16 + tz * 4 + ty], stores[kind].at[own_part + i]
            if away:
                remote(src, dst, send_kv, got_direct.at[kind, i // 4], device(x, ty, tz, c)).start()
            else:
                pltpu.make_async_copy(src, dst, got_direct.at[kind, 0]).start()

        return step

    def send_far(kind, ref):
        def step(i, away):
            ty, tz = target(i)
            src, dst = ref.at[(1 - pair) * 16 + tz * 4 + ty], stores[kind].at[own_part + i]
            remote(src, dst, send_kv, got_direct.at[kind, i // 4], device(beside, ty, tz, c)).start()

        return step

    def send_own_queries(i, away):
        ty, tz = target(i)
        src = q_ref.at[pair * 16 + tz * 4 + ty]
        if away:
            remote(src, queries.at[i], send_kv, got_queries.at[i // 4], device(x, ty, tz, c)).start()
        else:
            pltpu.make_async_copy(src, queries.at[0], got_queries.at[0]).start()

    def send_far_queries(i, away):
        ty, tz = target(i)
        src = q_ref.at[(1 - pair) * 16 + tz * 4 + ty]
        remote(src, queries.at[16 + i], send_kv, got_queries.at[4 + i // 4], device(beside, ty, tz, c)).start()

    def offsets(first, last, *steps):
        if first == 0:
            for step in steps:
                step(0, False)

        def body(i, carry):
            for step in steps:
                step(i, True)
            return carry

        lax.fori_loop(max(first, 1), last, body, 0)

    stores = (own_k, own_v, far_k, far_v)
    arriving = (own_part, own_part, far_part, far_part)
    relaying = (far_part, far_part, own_part, own_part)
    pltpu.make_async_copy(lists_out.at[own_head], lists_in.at[0], got_lists).start()
    pl.semaphore_wait(barrier, 33)
    offsets(0, 16, send_own(OWN_K, k_ref))

    def arrived(view, sem):
        pltpu.make_async_copy(view, view, sem).wait()

    def pass_on(kind, j):
        view = stores[kind].at[pl.ds(arriving[kind] + j * 4, 4)]
        arrived(view, got_direct.at[kind, j])
        remote(view, view, send_fwd, got_partner.at[kind], partner).start()
        if j == 3:
            part = stores[kind].at[pl.ds(arriving[kind], 16)]
            remote(part, part, send_fwd, got_sibling.at[kind], sibling).start()

    def relay(kind):
        part = stores[kind].at[pl.ds(relaying[kind], 16)]
        arrived(part, got_partner.at[kind])
        remote(part, part, send_fwd, got_relayed.at[kind], sibling).start()

    def complete(kind):
        view = stores[kind].at[pl.ds(0, 16)]
        arrived(view, got_sibling.at[kind])
        arrived(view, got_relayed.at[kind])

    def attend(kind, weights, settle, events):
        def one(unit):
            query = queries[unit]
            running, found = None, []
            for cols in COLS:
                keys = jnp.concatenate([stores[kind][lists[unit, 0, bases[kind] + col]] for col in cols], 0)
                found.append(lax.dot_general(query, keys, NT, preferred_element_type=jnp.float32))
                for n in range(len(cols)):
                    piece = found[-1][:, n * BAND : (n + 1) * BAND]
                    running = piece if running is None else jnp.maximum(running, piece)
            shift = settle(unit, jnp.broadcast_to(jnp.max(running, -1, keepdims=True) * SCALE, (BAND, BAND)))
            for cols, score in zip(COLS, found):
                weight = jnp.exp2(score * SCALE - jnp.concatenate([shift] * len(cols), 1))
                weights[unit, :, pl.ds(cols[0] * BAND, len(cols) * BAND)] = weight.astype(jnp.bfloat16)

        units(one, events)

    def mix(kind, weights, finish, events, after=None):
        def one(unit):
            acc = None
            for cols in COLS:
                values = jnp.concatenate([stores[kind][lists[unit, 0, bases[kind] + col]] for col in cols], 0)
                values = jnp.concatenate([values, jnp.ones_like(values)], 1)
                weight = weights[unit, :, pl.ds(cols[0] * BAND, len(cols) * BAND)]
                product = jnp.dot(weight, values, preferred_element_type=jnp.float32)
                acc = product if acc is None else acc + product
            finish(unit, acc)

        units(one, events, after)

    def units(one, events, after=None):
        def body(i, carry):
            for at, event in events:
                pl.when(i == at)(event)
            if after is None:
                mine = [i * STEP + n for n in range(STEP)]
            else:
                mine = [i * (STEP // 2) + n // 2 + 16 * (1 - n % 2) for n in range(STEP)]
            for unit in mine:
                one(unit)
            if after is not None:
                for unit in mine:
                    after(unit)
            return carry

        lax.fori_loop(0, 32 // STEP, body, 0)

    def passing(at, kind, j):
        return at, functools.partial(pass_on, kind, j)

    def relaying_at(at, kind):
        return at, functools.partial(relay, kind)

    bases = (pair * PER, pair * PER, (1 - pair) * PER, (1 - pair) * PER)

    def after_chunks(kind, *steps):
        for j in range(4):
            pass_on(kind, j)
            offsets(4 * j, 4 * j + 4, *steps)

    after_chunks(OWN_K, send_far(FAR_K, k_ref), send_own_queries)
    offsets(0, 16, send_lists_to)

    def next_far_keys(j):
        pass_on(FAR_K, j)
        offsets(4 * j, 4 * j + 4, send_far_queries, send_own(OWN_V, v_ref))

    def next_own_values(j):
        pass_on(OWN_V, j)
        offsets(4 * j, 4 * j + 4, send_far(FAR_V, v_ref))

    def query_chunk(j):
        arrived(queries.at[pl.ds(j * 4, 4)], got_queries.at[j])

    def querying(at, j):
        return at, functools.partial(query_chunk, j)

    next_far_keys(0)
    next_far_keys(1)
    arrived(lists_in, got_lists)
    copy_lists = pltpu.make_async_copy(lists_in, lists, lists_sem)
    copy_lists.start()
    relay(OWN_K)
    next_far_keys(2)
    copy_lists.wait()
    query_chunk(0)
    query_chunk(1)
    complete(OWN_K)

    def settle_own(unit, shift):
        max_own[unit] = shift
        return shift

    def settle_far(unit, shift):
        joint = jnp.maximum(shift, max_own[unit])
        max_own[unit] = jnp.exp2(max_own[unit] - joint)
        return joint

    attend(
        OWN_K,
        weights_own,
        settle_own,
        [
            (0, functools.partial(next_far_keys, 3)), querying(1, 2), querying(1, 3),
            (1, functools.partial(next_own_values, 0)), (1, functools.partial(next_own_values, 1)),
            (2, functools.partial(next_own_values, 2)), querying(2, 4), querying(2, 5),
            (3, functools.partial(next_own_values, 3)), querying(3, 6), querying(3, 7),
        ],
    )
    pass_on(FAR_V, 0)
    relay(FAR_K)
    complete(FAR_K)
    attend(
        FAR_K,
        weights_far,
        settle_far,
        [
            passing(1, FAR_V, 1), passing(1, FAR_V, 2), passing(2, FAR_V, 3), relaying_at(3, OWN_V),
        ],
    )
    complete(OWN_V)

    def keep(unit, acc):
        factor = max_own[unit]
        acc_own[unit] = (acc[:, :WIDTH] * factor).astype(jnp.bfloat16)
        max_own[unit] = acc[:, WIDTH:] * factor

    mix(OWN_V, weights_own, keep, [])
    relay(FAR_V)
    complete(FAR_V)

    def merge(unit, acc):
        top, bottom = acc[:, :WIDTH] + acc_own[unit].astype(jnp.float32), acc[:, WIDTH:] + max_own[unit]
        queries[unit] = (top / bottom).astype(jnp.bfloat16)

    def give_back(unit):
        i = unit % 16
        dy = i % 4
        dz = (i // 4 + dy) % 4
        plane = jnp.where(unit < 16, x, beside)

        @pl.when(unit == 0)
        def _():
            pltpu.make_async_copy(queries.at[0], o_ref.at[own_head], got_out).start()

        @pl.when(unit != 0)
        def _():
            remote(
                queries.at[unit], o_ref.at[own_head], send_out, got_out,
                device(plane, (y - dy + 4) % 4, (z - dz + 4) % 4, c),
            ).start()

    mix(FAR_V, weights_far, merge, [], give_back)

    def sent(view, sem):
        pltpu.make_async_copy(view, view, sem).wait()

    arrived(o_ref, got_out)
    sent(o_ref.at[pl.ds(0, 31)], send_out)
    sent(lists_out.at[pl.ds(0, 31)], send_lists)
    for store in stores[:2]:
        sent(store.at[pl.ds(0, 31)], send_kv)
    sent(queries.at[pl.ds(0, 31)], send_kv)
    for store in stores:
        sent(store.at[pl.ds(0, 48)], send_fwd)


def on_device(queries, keys, values, tiles):
    dma = pltpu.SemaphoreType.DMA
    any_space = pl.BlockSpec(memory_space=pl.ANY)
    bf16, f32 = jnp.bfloat16, jnp.float32
    return pl.pallas_call(
        kernel,
        out_shape=jax.ShapeDtypeStruct((HEADS, BAND, WIDTH), bf16),
        in_specs=[any_space, any_space, any_space, pl.BlockSpec(memory_space=pltpu.VMEM)],
        out_specs=any_space,
        scratch_shapes=[
            pltpu.VMEM((64, BAND, WIDTH), bf16),
            pltpu.VMEM((64, BAND, WIDTH), bf16),
            pltpu.VMEM((64, BAND, WIDTH), bf16),
            pltpu.VMEM((64, BAND, WIDTH), bf16),
            pltpu.VMEM((32, BAND, WIDTH), bf16),
            pltpu.VMEM((HEADS, 1, 128), jnp.int32),
            pltpu.VMEM((32, 1, 128), jnp.int32),
            pltpu.SMEM((32, 1, 128), jnp.int32),
            pltpu.VMEM((32, BAND, PER * BAND), bf16),
            pltpu.VMEM((32, BAND, PER * BAND), bf16),
            pltpu.VMEM((32, BAND, WIDTH), bf16),
            pltpu.VMEM((32, BAND, BAND), f32),
            dma, dma, dma, dma,
            dma((4, 4)), dma((4,)), dma((4,)), dma((4,)), dma((8,)), dma, dma, dma,
        ],
        compiler_params=pltpu.CompilerParams(collective_id=0, has_side_effects=True, vmem_limit_bytes=52 * 2**20),
        cost_estimate=pl.CostEstimate(flops=10_200_000_000, bytes_accessed=4 * 2**20, transcendentals=20_000_000),
        name="attend_listed",
    )(queries, keys, values, tiles)


def solution(mesh):
    return jax.shard_map(
        on_device,
        mesh=mesh,
        in_specs=(
            P(None, ("grp", "seq"), None),
            P(None, ("grp", "seq"), None),
            P(None, ("grp", "seq"), None),
            P(("grp", "seq"), None, None),
        ),
        out_specs=P(None, ("grp", "seq"), None),
        check_vma=False,
    )
```

```python
import functools

import jax
import jax.numpy as jnp
from jax import lax
from jax.experimental import pallas as pl
from jax.experimental.pallas import tpu as pltpu
from jax.sharding import PartitionSpec as P

MESH = pl.DeviceIdType.MESH
BAND = 128
WIDTH = 128
HEADS = 32
PER = 19
SCALE = 128.0**-0.5 * 1.4426950408889634
NT = (((1,), (1,)), ((), ()))
OWN_K, OWN_V, FAR_K, FAR_V = range(4)
STEP = 8
COLS = [list(range(i, min(PER, i + 2))) for i in range(0, PER, 2)]


def device(x, y, z, c):
    return (x // 2, ((z * 2 + x % 2) * 4 + y) * 2 + c)


def kernel(
    q_ref, k_ref, v_ref, tiles_ref, o_ref,
    own_k, own_v, far_k, far_v, queries, lists_out, lists_in, lists, weights_own, weights_far, acc_own, max_own,
    send_kv, send_lists, send_fwd, send_out,
    got_direct, got_partner, got_sibling, got_relayed, got_queries, got_lists, got_out, lists_sem,
):
    s = lax.axis_index("seq")
    pair = lax.axis_index("grp")
    c = s % 2
    y = (s // 2) % 4
    x_lo = (s // 8) % 2
    z = s // 16
    x = pair * 2 + x_lo
    beside = 3 - x
    sibling = device(x, y, z, 1 - c)
    partner = device(x + 1 - 2 * x_lo, y, z, c)
    own_head = pair * 16 + z * 4 + y
    own_part = (x_lo * 2 + c) * 16
    far_part = ((1 - x_lo) * 2 + c) * 16

    def target(i):
        dy = i % 4
        dz = (i // 4 + dy) % 4
        return (y + dy) % 4, (z + dz) % 4

    barrier = pltpu.get_barrier_semaphore()

    def greet(device_id):
        pl.semaphore_signal(barrier, inc=1, device_id=device_id, device_id_type=MESH)

    greet(sibling)
    greet(partner)
    greet(device(beside, y, z, c))

    def greet_both(i, carry):
        ty, tz = target(i)
        greet(device(x, ty, tz, c))
        greet(device(beside, ty, tz, c))
        return carry

    lax.fori_loop(1, 16, greet_both, 0)

    t = tiles_ref[0]
    head = lax.broadcasted_iota(jnp.int32, t.shape, 0)
    dy_of = ((head & 3) - ((t >> 1) & 3)) & 3
    dz_of = (((head >> 2) & 3) - ((t >> 4) & 3)) & 3
    slot_of = (((t >> 3) & 1) * 2 + (t & 1)) * 16 + ((dz_of - dy_of) & 3) * 4 + dy_of
    slot_of = jnp.concatenate([slot_of, jnp.zeros((HEADS, 128 - 2 * PER), jnp.int32)], 1)
    for h in range(HEADS):
        lists_out[h] = slot_of[h : h + 1]

    def remote(src, dst, send_sem, recv_sem, device_id):
        return pltpu.make_async_remote_copy(
            src_ref=src, dst_ref=dst, send_sem=send_sem, recv_sem=recv_sem, device_id=device_id, device_id_type=MESH
        )

    def send_lists_to(i, away):
        ty, tz = target(i)
        if away:
            remote(
                lists_out.at[pair * 16 + tz * 4 + ty], lists_in.at[i], send_lists, got_lists, device(x, ty, tz, c)
            ).start()
        remote(
            lists_out.at[(1 - pair) * 16 + tz * 4 + ty], lists_in.at[16 + i], send_lists, got_lists, device(beside, ty, tz, c)
        ).start()

    def send_own(kind, ref):
        def step(i, away):
            ty, tz = target(i)
            src, dst = ref.at[pair * 16 + tz * 4 + ty], stores[kind].at[own_part + i]
            if away:
                remote(src, dst, send_kv, got_direct.at[kind, i // 4], device(x, ty, tz, c)).start()
            else:
                pltpu.make_async_copy(src, dst, got_direct.at[kind, 0]).start()

        return step

    def send_far(kind, ref):
        def step(i, away):
            ty, tz = target(i)
            src, dst = ref.at[(1 - pair) * 16 + tz * 4 + ty], stores[kind].at[own_part + i]
            remote(src, dst, send_kv, got_direct.at[kind, i // 4], device(beside, ty, tz, c)).start()

        return step

    def send_own_queries(i, away):
        ty, tz = target(i)
        src = q_ref.at[pair * 16 + tz * 4 + ty]
        if away:
            remote(src, queries.at[i], send_kv, got_queries.at[i // 4], device(x, ty, tz, c)).start()
        else:
            pltpu.make_async_copy(src, queries.at[0], got_queries.at[0]).start()

    def send_far_queries(i, away):
        ty, tz = target(i)
        src = q_ref.at[(1 - pair) * 16 + tz * 4 + ty]
        remote(src, queries.at[16 + i], send_kv, got_queries.at[4 + i // 4], device(beside, ty, tz, c)).start()

    def offsets(first, last, *steps):
        if first == 0:
            for step in steps:
                step(0, False)

        def body(i, carry):
            for step in steps:
                step(i, True)
            return carry

        lax.fori_loop(max(first, 1), last, body, 0)

    stores = (own_k, own_v, far_k, far_v)
    arriving = (own_part, own_part, far_part, far_part)
    relaying = (far_part, far_part, own_part, own_part)
    pltpu.make_async_copy(lists_out.at[own_head], lists_in.at[0], got_lists).start()
    pl.semaphore_wait(barrier, 33)
    offsets(0, 16, send_own(OWN_K, k_ref))

    def arrived(view, sem):
        pltpu.make_async_copy(view, view, sem).wait()

    def pass_on(kind, j):
        view = stores[kind].at[pl.ds(arriving[kind] + j * 4, 4)]
        arrived(view, got_direct.at[kind, j])
        remote(view, view, send_fwd, got_partner.at[kind], partner).start()
        if j == 3:
            part = stores[kind].at[pl.ds(arriving[kind], 16)]
            remote(part, part, send_fwd, got_sibling.at[kind], sibling).start()

    def relay(kind):
        part = stores[kind].at[pl.ds(relaying[kind], 16)]
        arrived(part, got_partner.at[kind])
        remote(part, part, send_fwd, got_relayed.at[kind], sibling).start()

    def complete(kind):
        view = stores[kind].at[pl.ds(0, 16)]
        arrived(view, got_sibling.at[kind])
        arrived(view, got_relayed.at[kind])

    def attend(kind, weights, settle, events):
        def one(unit):
            query = queries[unit]
            running, found = None, []
            for cols in COLS:
                keys = jnp.concatenate([stores[kind][lists[unit, 0, bases[kind] + col]] for col in cols], 0)
                found.append(lax.dot_general(query, keys, NT, preferred_element_type=jnp.float32))
                for n in range(len(cols)):
                    piece = found[-1][:, n * BAND : (n + 1) * BAND]
                    running = piece if running is None else jnp.maximum(running, piece)
            shift = settle(unit, jnp.broadcast_to(jnp.max(running, -1, keepdims=True) * SCALE, (BAND, BAND)))
            for cols, score in zip(COLS, found):
                weight = jnp.exp2(score * SCALE - jnp.concatenate([shift] * len(cols), 1))
                weights[unit, :, pl.ds(cols[0] * BAND, len(cols) * BAND)] = weight.astype(jnp.bfloat16)

        units(one, events)

    def mix(kind, weights, finish, events, after=None):
        def one(unit):
            acc = None
            for cols in COLS:
                values = jnp.concatenate([stores[kind][lists[unit, 0, bases[kind] + col]] for col in cols], 0)
                values = jnp.concatenate([values, jnp.ones_like(values)], 1)
                weight = weights[unit, :, pl.ds(cols[0] * BAND, len(cols) * BAND)]
                product = jnp.dot(weight, values, preferred_element_type=jnp.float32)
                acc = product if acc is None else acc + product
            finish(unit, acc)

        units(one, events, after)

    def units(one, events, after=None):
        step = STEP if after is None else STEP // 2

        def body(i, carry):
            for at, event in events:
                pl.when(i == at)(event)
            if after is None:
                mine = [i * STEP + n for n in range(STEP)]
            else:
                mine = [i * (step // 2) + n // 2 + 16 * (1 - n % 2) for n in range(step)]
            for unit in mine:
                one(unit)
            if after is not None:
                for unit in mine:
                    after(unit)
            return carry

        lax.fori_loop(0, 32 // step, body, 0)

    def passing(at, kind, j):
        return at, functools.partial(pass_on, kind, j)

    def relaying_at(at, kind):
        return at, functools.partial(relay, kind)

    bases = (pair * PER, pair * PER, (1 - pair) * PER, (1 - pair) * PER)

    def after_chunks(kind, *steps):
        for j in range(4):
            pass_on(kind, j)
            offsets(4 * j, 4 * j + 4, *steps)

    after_chunks(OWN_K, send_far(FAR_K, k_ref), send_own_queries)
    offsets(0, 16, send_lists_to)

    def next_far_keys(j):
        pass_on(FAR_K, j)
        offsets(4 * j, 4 * j + 4, send_far_queries, send_own(OWN_V, v_ref))

    def next_own_values(j):
        pass_on(OWN_V, j)
        offsets(4 * j, 4 * j + 4, send_far(FAR_V, v_ref))

    def query_chunk(j):
        arrived(queries.at[pl.ds(j * 4, 4)], got_queries.at[j])

    def querying(at, j):
        return at, functools.partial(query_chunk, j)

    next_far_keys(0)
    next_far_keys(1)
    arrived(lists_in, got_lists)
    copy_lists = pltpu.make_async_copy(lists_in, lists, lists_sem)
    copy_lists.start()
    relay(OWN_K)
    next_far_keys(2)
    copy_lists.wait()
    query_chunk(0)
    query_chunk(1)
    complete(OWN_K)

    def settle_own(unit, shift):
        max_own[unit] = shift
        return shift

    def settle_far(unit, shift):
        joint = jnp.maximum(shift, max_own[unit])
        max_own[unit] = jnp.exp2(max_own[unit] - joint)
        return joint

    attend(
        OWN_K,
        weights_own,
        settle_own,
        [
            (0, functools.partial(next_far_keys, 3)), querying(1, 2), querying(1, 3),
            (1, functools.partial(next_own_values, 0)), (1, functools.partial(next_own_values, 1)),
            (2, functools.partial(next_own_values, 2)), querying(2, 4), querying(2, 5),
            (3, functools.partial(next_own_values, 3)), querying(3, 6), querying(3, 7),
        ],
    )
    pass_on(FAR_V, 0)
    relay(FAR_K)
    complete(FAR_K)
    attend(
        FAR_K,
        weights_far,
        settle_far,
        [
            passing(1, FAR_V, 1), passing(1, FAR_V, 2), passing(2, FAR_V, 3), relaying_at(3, OWN_V),
        ],
    )
    complete(OWN_V)

    def keep(unit, acc):
        factor = max_own[unit]
        acc_own[unit] = (acc[:, :WIDTH] * factor).astype(jnp.bfloat16)
        max_own[unit] = acc[:, WIDTH:] * factor

    mix(OWN_V, weights_own, keep, [])
    relay(FAR_V)
    complete(FAR_V)

    def merge(unit, acc):
        top, bottom = acc[:, :WIDTH] + acc_own[unit].astype(jnp.float32), acc[:, WIDTH:] + max_own[unit]
        queries[unit] = (top / bottom).astype(jnp.bfloat16)

    def give_back(unit):
        i = unit % 16
        dy = i % 4
        dz = (i // 4 + dy) % 4
        plane = jnp.where(unit < 16, x, beside)

        @pl.when(unit == 0)
        def _():
            pltpu.make_async_copy(queries.at[0], o_ref.at[own_head], got_out).start()

        @pl.when(unit != 0)
        def _():
            remote(
                queries.at[unit], o_ref.at[own_head], send_out, got_out,
                device(plane, (y - dy + 4) % 4, (z - dz + 4) % 4, c),
            ).start()

    mix(FAR_V, weights_far, merge, [], give_back)

    def sent(view, sem):
        pltpu.make_async_copy(view, view, sem).wait()

    arrived(o_ref, got_out)
    sent(o_ref.at[pl.ds(0, 31)], send_out)
    sent(lists_out.at[pl.ds(0, 31)], send_lists)
    for store in stores[:2]:
        sent(store.at[pl.ds(0, 31)], send_kv)
    sent(queries.at[pl.ds(0, 31)], send_kv)
    for store in stores:
        sent(store.at[pl.ds(0, 48)], send_fwd)


def on_device(queries, keys, values, tiles):
    dma = pltpu.SemaphoreType.DMA
    any_space = pl.BlockSpec(memory_space=pl.ANY)
    bf16, f32 = jnp.bfloat16, jnp.float32
    return pl.pallas_call(
        kernel,
        out_shape=jax.ShapeDtypeStruct((HEADS, BAND, WIDTH), bf16),
        in_specs=[any_space, any_space, any_space, pl.BlockSpec(memory_space=pltpu.VMEM)],
        out_specs=any_space,
        scratch_shapes=[
            pltpu.VMEM((64, BAND, WIDTH), bf16),
            pltpu.VMEM((64, BAND, WIDTH), bf16),
            pltpu.VMEM((64, BAND, WIDTH), bf16),
            pltpu.VMEM((64, BAND, WIDTH), bf16),
            pltpu.VMEM((32, BAND, WIDTH), bf16),
            pltpu.VMEM((HEADS, 1, 128), jnp.int32),
            pltpu.VMEM((32, 1, 128), jnp.int32),
            pltpu.SMEM((32, 1, 128), jnp.int32),
            pltpu.VMEM((32, BAND, PER * BAND), bf16),
            pltpu.VMEM((32, BAND, PER * BAND), bf16),
            pltpu.VMEM((32, BAND, WIDTH), bf16),
            pltpu.VMEM((32, BAND, BAND), f32),
            dma, dma, dma, dma,
            dma((4, 4)), dma((4,)), dma((4,)), dma((4,)), dma((8,)), dma, dma, dma,
        ],
        compiler_params=pltpu.CompilerParams(collective_id=0, has_side_effects=True, vmem_limit_bytes=52 * 2**20),
        cost_estimate=pl.CostEstimate(flops=10_200_000_000, bytes_accessed=4 * 2**20, transcendentals=20_000_000),
        name="attend_listed",
    )(queries, keys, values, tiles)


def solution(mesh):
    return jax.shard_map(
        on_device,
        mesh=mesh,
        in_specs=(
            P(None, ("grp", "seq"), None),
            P(None, ("grp", "seq"), None),
            P(None, ("grp", "seq"), None),
            P(("grp", "seq"), None, None),
        ),
        out_specs=P(None, ("grp", "seq"), None),
        check_vma=False,
    )
```
